32 devices in a mesh: box: 8 (over z, core), dir: 4 (over y, x).
Axes of the slice: x: 2, y: 2, z: 4, core: 2. Of those that a mesh axis runs over, the one named last changes fastest.
Arguments:
- currents: float32 [4096, 2, 128], P(('box', 'dir')), may hold values from -6 to 6
- near_blocks: float32 [16, 2, 128, 128], replicated, may hold values from -0.078125 to 0.078125
- block_ids: int32 [4096, 27], P(('box', 'dir')), may hold values from 0 to 15
- neighbors: int32 [4096, 27], P(('box', 'dir')), may hold values from 0 to 4095, as said below
- leaf_place: int32 [4096, 2], P(('box', 'dir')), may hold values from 0 to 255, as said below
- radiation: float32 [2, 128, 128], replicated, may hold values from -0.375 to 0.375
- interpolation: float32 [128, 8192], replicated, may hold values from -0.5 to 0.5
- translation: float32 [8192, 2, 316], P('dir'), may hold values from -0.625 to 0.625
- list_src: int32 [256, 40], replicated, may hold values from 0 to 255, as said below
- list_offset: int32 [256, 40], replicated, may hold values from 0 to 315
Outputs:
- product: float32 [4096, 2, 128], P(('box', 'dir'))
The draws below stay inside these ranges and needn't reach their ends.
Inputs may be any that keep to these rules, and one draw needn't show every extreme that they name: `neighbors`: the neighbours of a leaf stored on device i (devices numbered over box, then dir) are stored on device i - 1, i or i + 1. `leaf_place`: the parent of a leaf stored on a device of box index b is one of the 32 coarse boxes b * 32 to (b + 1) * 32 - 1 owned by b; the position code lies in 0 to 63. `list_src`: coarse box c belongs to box index c // 32; for every pair of box indices b, p the lists of b's coarse boxes name exactly 8 distinct coarse boxes of p.
All inputs are finite; a program needn't handle non-finite values.
Results may differ from the reference program's by a relative error of at most 0.0003.
Values sent between devices are 32-bit elements; how exact they have to be, the bound alone decides.
A program may use at most 128 MiB of HBM per device.

```python
import math
import jax
import jax.numpy as jnp
from jax import lax

NU = 128
K0 = 128
NBLK = 16
NB = 27
NOFF = 316
IL = 40
LEAF_DEV = 128
CB_DEV = 32
NEED = 8
K1 = 8192
NLEAF = 4096
NCB = 256
N_BOX = 8
N_DIR = 4


def draw_neighbors(key, part):
    key = jax.random.fold_in(key, 11)
    key_step, key_slot = jax.random.split(key)
    leaf = jnp.arange(NLEAF, dtype=jnp.int32)
    device = leaf // LEAF_DEV
    devices = NLEAF // LEAF_DEV
    step = jax.random.randint(key_step, (NLEAF, NB), -1, 2)
    other = jnp.clip(device[:, None] + step, 0, devices - 1)
    slot = jax.random.randint(key_slot, (NLEAF, NB), 0, LEAF_DEV)
    return (other * LEAF_DEV + slot).astype(jnp.int32)


def draw_leaf_place(key, part):
    key = jax.random.fold_in(key, 17)
    key_parent, key_pos = jax.random.split(key)
    leaf = jnp.arange(NLEAF, dtype=jnp.int32)
    owner = leaf // (LEAF_DEV * N_DIR)
    parent = owner * CB_DEV + jax.random.randint(key_parent, (NLEAF,), 0, CB_DEV)
    position = jax.random.randint(key_pos, (NLEAF,), 0, 64)
    return jnp.stack([parent, position], 1).astype(jnp.int32)


def draw_list_src(key, part):
    key = jax.random.fold_in(key, 23)
    key_pick, key_extra, key_order = jax.random.split(key, 3)
    boxes = NCB // CB_DEV
    entries = CB_DEV * IL
    pick_keys = jax.random.split(key_pick, boxes * boxes)
    chosen = jax.vmap(lambda k: jax.random.permutation(k, CB_DEV)[:NEED])(pick_keys).reshape(boxes, boxes, NEED)
    cover = jnp.broadcast_to(jnp.arange(boxes * NEED, dtype=jnp.int32), (boxes, boxes * NEED))
    extra = jax.random.randint(key_extra, (boxes, entries - boxes * NEED), 0, boxes * NEED)
    pairs = jnp.concatenate([cover, extra], 1)
    order_keys = jax.random.split(key_order, boxes)
    pairs = jax.vmap(lambda k, row: jax.random.permutation(k, row))(order_keys, pairs)
    peer = pairs // NEED
    slot = pairs % NEED
    receiver = jnp.arange(boxes, dtype=jnp.int32)[:, None]
    source = peer * CB_DEV + chosen[receiver, peer, slot]
    return source.reshape(NCB, IL).astype(jnp.int32)


def set_ends(values, stream_key, least, top_value):
    longest = values.shape.index(max(values.shape))
    spots = []
    for shift in (0, 1):
        where = [jax.random.randint(jax.random.fold_in(stream_key, axis), (), 0, length) for axis, length in enumerate(values.shape)]
        where[longest] = (where[longest] + shift) % values.shape[longest]
        spots.append(tuple(where))
    return values.at[spots[0]].set(least).at[spots[1]].set(top_value)


def block_levels(stream_key, shape, shards, low, top_value):
    def one(dim, parts):
        steps = jax.random.uniform(jax.random.fold_in(jax.random.fold_in(stream_key, 6), dim), (parts,), jnp.float32, low / len(shards), top_value / len(shards))
        return jnp.repeat(jnp.exp(steps), shape[dim] // parts).reshape((-1,) + (1,) * (len(shape) - dim - 1))

    level = one(*shards[0])
    for cut in shards[1:]:
        level = level * one(*cut)
    return level


def scatter_about(rng, dims, scale, most, pieces=(), kind=jnp.bfloat16):
    values = jax.random.normal(rng, dims, jnp.float32) * scale
    if len(pieces) > 0:
        values = block_levels(rng, dims, pieces, -0.22, 0.18) * values
    return jnp.clip(values, min=-most, max=most).astype(kind)


def setup_inputs(seed: int = 0) -> dict:
    splits = jax.random.split(jax.random.key(seed), 11)
    currents = scatter_about(splits[0], (NLEAF, 2, NU), 1.0, 6.0, ((0, 32),), jnp.float32)
    near_blocks = scatter_about(splits[1], (NBLK, 2, NU, NU), (2 * NU * NB) ** -0.5, 0.078125, (), jnp.float32)
    block_ids = set_ends(jax.random.randint(splits[2], (NLEAF, NB), 0, NBLK), jax.random.fold_in(splits[2], 1), 0, NBLK - 1).astype(jnp.int32)
    neighbors = draw_neighbors(jax.random.fold_in(splits[10], 71), 0)
    leaf_place = draw_leaf_place(jax.random.fold_in(splits[10], 71), 0)
    radiation = scatter_about(splits[5], (2, NU, K0), (2 * NU) ** -0.5, 0.375, (), jnp.float32)
    interpolation = scatter_about(splits[6], (K0, K1), K0 ** -0.5, 0.5, (), jnp.float32)
    translation = scatter_about(splits[7], (K1, 2, NOFF), (0.25 / IL ** 0.5), 0.625, ((0, 4),), jnp.float32)
    list_src = draw_list_src(jax.random.fold_in(splits[10], 71), 0)
    list_offset = set_ends(jax.random.randint(splits[9], (NCB, IL), 0, NOFF), jax.random.fold_in(splits[9], 1), 0, NOFF - 1).astype(jnp.int32)
    return dict(currents=currents, near_blocks=near_blocks, block_ids=block_ids, neighbors=neighbors, leaf_place=leaf_place, radiation=radiation, interpolation=interpolation, translation=translation, list_src=list_src, list_offset=list_offset)


kappa_leaf = math.pi
highest = lax.Precision.HIGHEST

def matmul(left, right):
    return jnp.dot(left, right, precision=highest, preferred_element_type=jnp.float32)

def phases(position, start, count, polar):
    order = start + jnp.arange(count, dtype=jnp.int32)
    cycle = order // (2 * polar)
    beside_all = order % (2 * polar)
    theta = math.pi * (cycle.astype(jnp.float32) + 0.5) / polar
    azimuth = math.pi * beside_all.astype(jnp.float32) / polar
    along_x = jnp.sin(theta) * jnp.cos(azimuth)
    along_y = jnp.sin(theta) * jnp.sin(azimuth)
    along_z = jnp.cos(theta)
    off_x = (position % 4).astype(jnp.float32) - 1.5
    off_y = (position // 4 % 4).astype(jnp.float32) - 1.5
    off_z = (position // 16).astype(jnp.float32) - 1.5
    angle = kappa_leaf * (off_x[:, None] * along_x[None, :] + off_y[:, None] * along_y[None, :] + off_z[:, None] * along_z[None, :])
    return (jnp.cos(angle), jnp.sin(angle), jnp.sin(theta))

def near_field(gathered, local, kinds, near_blocks):
    rows = jnp.take(gathered, local, axis=0)
    count = near_blocks.shape[0]
    onehot = (kinds[..., None] == jnp.arange(count, dtype=jnp.int32)).astype(jnp.float32)
    summed = jnp.einsum('ljt,ljrn->trln', onehot, rows, precision=highest)
    block_r = near_blocks[:, 0]
    block_i = near_blocks[:, 1]
    real = jnp.einsum('tmn,tln->lm', block_r, summed[:, 0], precision=highest) - jnp.einsum('tmn,tln->lm', block_i, summed[:, 1], precision=highest)
    imag = jnp.einsum('tmn,tln->lm', block_r, summed[:, 1], precision=highest) + jnp.einsum('tmn,tln->lm', block_i, summed[:, 0], precision=highest)
    return jnp.stack([real, imag], 1)

def radiate(cur, radiation):
    real = matmul(cur[:, 0], radiation[0]) - matmul(cur[:, 1], radiation[1])
    imag = matmul(cur[:, 0], radiation[1]) + matmul(cur[:, 1], radiation[0])
    return (real, imag)

def receive(real, imag, radiation):
    out_r = matmul(real, radiation[0].T) + matmul(imag, radiation[1].T)
    out_i = matmul(imag, radiation[0].T) - matmul(real, radiation[1].T)
    return jnp.stack([out_r, out_i], 1)

def reference(currents, near_blocks, block_ids, neighbors, leaf_place, radiation, interpolation, translation, list_src, list_offset):
    count_k1 = interpolation.shape[1]
    polar = math.isqrt(count_k1 // 2)
    scale = math.sqrt(interpolation.shape[0] / count_k1)
    group = LEAF_DEV * N_DIR
    total = NCB
    cur_g = currents.reshape(N_BOX, group, 2, NU)
    place_g = leaf_place.reshape(N_BOX, group, 2)
    near_g = neighbors.reshape(N_BOX, group, NB)
    kinds_g = block_ids.reshape(N_BOX, group, NB)

    def gather_out(acc, item):
        cur, place = item
        s_r, s_i = radiate(cur, radiation)
        wave_r = matmul(s_r, interpolation)
        wave_i = matmul(s_i, interpolation)
        cosine, sine, unused = phases(place[:, 1], 0, count_k1, polar)
        shift_r = wave_r * cosine + wave_i * sine
        shift_i = wave_i * cosine - wave_r * sine
        acc = acc + jax.ops.segment_sum(jnp.stack([shift_r, shift_i], 1), place[:, 0], num_segments=total)
        return (acc, None)
    coarse = lax.scan(gather_out, jnp.zeros((total, 2, count_k1), jnp.float32), (cur_g, place_g))[0]

    def translate(acc, entry):
        source_ids, offsets = entry
        source = jnp.take(coarse, source_ids, axis=0)
        table = jnp.transpose(jnp.take(translation, offsets, axis=2), (2, 1, 0))
        real = table[:, 0] * source[:, 0] - table[:, 1] * source[:, 1]
        imag = table[:, 0] * source[:, 1] + table[:, 1] * source[:, 0]
        return (acc + jnp.stack([real, imag], 1), None)
    fields = lax.scan(translate, jnp.zeros((total, 2, count_k1), jnp.float32), (list_src.T, list_offset.T))[0]

    def spread(carry, item):
        place, near_ids, kinds = item
        near = near_field(currents, near_ids, kinds, near_blocks)
        field = jnp.take(fields, place[:, 0], axis=0)
        cosine, sine, polar_sine = phases(place[:, 1], 0, count_k1, polar)
        weight = polar_sine * scale
        back_r = (field[:, 0] * cosine - field[:, 1] * sine) * weight
        back_i = (field[:, 0] * sine + field[:, 1] * cosine) * weight
        far = receive(matmul(back_r, interpolation.T), matmul(back_i, interpolation.T), radiation)
        return (carry, near + far)
    out = lax.scan(spread, jnp.zeros((), jnp.float32), (place_g, near_g, kinds_g))[1]
    return out.reshape(NLEAF, 2, NU)
```

```python
import functools
import math

import jax
import jax.numpy as jnp
from jax import lax
from jax.experimental import pallas as pl
from jax.experimental.pallas import tpu as pltpu
from jax.sharding import PartitionSpec as P

kappa_leaf = math.pi
high = lax.Precision.HIGH
need = 8
MESH = pl.DeviceIdType.MESH


def padded(block, sides, width):
    for axis, dim in sides:
        count = lax.axis_size(axis)
        forward = [(i, i + 1) for i in range(count - 1)]
        backward = [(target, source) for source, target in forward]
        low = lax.ppermute(
            lax.slice_in_dim(block, block.shape[dim] - width, None, axis=dim), axis, forward
        )
        high_side = lax.ppermute(lax.slice_in_dim(block, 0, width, axis=dim), axis, backward)
        block = jnp.concatenate([low, block, high_side], axis=dim)
    return block


def matmul(left, right):
    return jnp.dot(left, right, precision=high, preferred_element_type=jnp.float32)


def exact_matmul(left, right):
    return jnp.dot(
        left.astype(jnp.bfloat16),
        right.astype(jnp.bfloat16),
        preferred_element_type=jnp.float32,
    )


def onehot(values, count, base=0):
    return ((values - base)[..., None] == jnp.arange(count, dtype=jnp.int32)).astype(jnp.float32)


def phase_table(start, count, polar):
    order = start + jnp.arange(count, dtype=jnp.int32)
    cycle = order // (2 * polar)
    beside_all = order % (2 * polar)
    theta = math.pi * (cycle.astype(jnp.float32) + 0.5) / polar
    azimuth = math.pi * beside_all.astype(jnp.float32) / polar
    along_x = jnp.sin(theta) * jnp.cos(azimuth)
    along_y = jnp.sin(theta) * jnp.sin(azimuth)
    along_z = jnp.cos(theta)
    position = jnp.arange(64, dtype=jnp.int32)
    off_x = (position % 4).astype(jnp.float32) - 1.5
    off_y = (position // 4 % 4).astype(jnp.float32) - 1.5
    off_z = (position // 16).astype(jnp.float32) - 1.5
    angle = kappa_leaf * (
        off_x[:, None] * along_x[None, :]
        + off_y[:, None] * along_y[None, :]
        + off_z[:, None] * along_z[None, :]
    )
    return (jnp.cos(angle), jnp.sin(angle), jnp.sin(theta))


def near_field(gathered, local, kinds, near_blocks):
    count = near_blocks.shape[0]
    leaves = local.shape[0]
    width = gathered.shape[0]
    pairs = jnp.einsum(
        "ljt,ljm->tlm",
        onehot(kinds, count).astype(jnp.bfloat16),
        onehot(local, width).astype(jnp.bfloat16),
        preferred_element_type=jnp.float32,
    )
    summed = matmul(pairs.reshape(count * leaves, width), gathered.reshape(width, -1))
    summed = summed.reshape(count, leaves, 2, -1)
    block_r = near_blocks[:, 0]
    block_i = near_blocks[:, 1]

    def apply(block, rows):
        return jnp.einsum("tmn,tln->lm", block, rows, precision=high)

    real = apply(block_r, summed[:, :, 0]) - apply(block_i, summed[:, :, 1])
    imag = apply(block_r, summed[:, :, 1]) + apply(block_i, summed[:, :, 0])
    return jnp.stack([real, imag], 1)


def radiate(cur, radiation):
    real = matmul(cur[:, 0], radiation[0]) - matmul(cur[:, 1], radiation[1])
    imag = matmul(cur[:, 0], radiation[1]) + matmul(cur[:, 1], radiation[0])
    return jnp.stack([real, imag], 1)


def receive(real, imag, radiation):
    out_r = matmul(real, radiation[0].T) + matmul(imag, radiation[1].T)
    out_i = matmul(imag, radiation[0].T) - matmul(real, radiation[1].T)
    return jnp.stack([out_r, out_i], 1)


def ranks(present):
    size = present.shape[1]
    order = jnp.arange(size)
    before = (order[:, None] < order[None, :]).astype(jnp.float32)
    return exact_matmul(present, before)


def exchange_kernel(
    peers, boxes, length, index_ref, off_ref, send_ref, table_ref, out_ref, held, send_sem, recv_sem
):
    me = lax.axis_index("box")
    barrier = pltpu.get_barrier_semaphore()
    for step in range(1, peers):
        other = lax.rem(me + step, peers)
        pl.semaphore_signal(barrier, inc=1, device_id={"box": other}, device_id_type=MESH)
    pl.semaphore_wait(barrier, peers - 1)
    copies = []
    for step in range(1, peers):
        other = lax.rem(me + step, peers)
        copy = pltpu.make_async_remote_copy(
            src_ref=send_ref.at[other],
            dst_ref=held.at[me],
            send_sem=send_sem.at[step],
            recv_sem=recv_sem.at[step],
            device_id={"box": other},
            device_id_type=MESH,
        )
        copy.start()
        copies.append(copy)
    held[me] = send_ref[me]
    for copy in copies:
        copy.wait()

    def one(box, carry):
        real = jnp.zeros(out_ref.shape[2:], jnp.float32)
        imag = jnp.zeros(out_ref.shape[2:], jnp.float32)

        def entry(item, total):
            real, imag = total
            source = index_ref[box * length + item]
            off = off_ref[box * length + item]
            src_r = held[source // need, source % need, 0]
            src_i = held[source // need, source % need, 1]
            tab_r = table_ref[off, 0]
            tab_i = table_ref[off, 1]
            real = real + (tab_r * src_r - tab_i * src_i)
            imag = imag + (tab_r * src_i + tab_i * src_r)
            return real, imag

        real, imag = lax.fori_loop(0, length, entry, (real, imag), unroll=8)
        out_ref[box, 0] = real
        out_ref[box, 1] = imag
        return carry

    lax.fori_loop(0, boxes, one, 0)


def exchange(send, table, index, offsets, boxes):
    peers = send.shape[0]
    length = index.shape[0] // boxes
    tail = send.shape[2:]
    return pl.pallas_call(
        functools.partial(exchange_kernel, peers, boxes, length),
        out_shape=jax.ShapeDtypeStruct((boxes,) + tail, jnp.float32),
        in_specs=[
            pl.BlockSpec(memory_space=pltpu.SMEM),
            pl.BlockSpec(memory_space=pltpu.SMEM),
            pl.BlockSpec(memory_space=pltpu.VMEM),
            pl.BlockSpec(memory_space=pltpu.VMEM),
        ],
        out_specs=pl.BlockSpec(memory_space=pltpu.VMEM),
        scratch_shapes=[
            pltpu.VMEM(send.shape, jnp.float32),
            pltpu.SemaphoreType.DMA((peers,)),
            pltpu.SemaphoreType.DMA((peers,)),
        ],
        compiler_params=pltpu.CompilerParams(
            collective_id=0, has_side_effects=True, vmem_limit_bytes=24 * 2**20
        ),
    )(index, offsets, send, table)


def on_device(
    currents,
    near_blocks,
    block_ids,
    neighbors,
    leaf_place,
    radiation,
    interpolation,
    translation,
    list_src,
    list_offset,
):
    leaf_count = currents.shape[0]
    count_k0 = interpolation.shape[0]
    count_k1 = interpolation.shape[1]
    polar = math.isqrt(count_k1 // 2)
    scale = math.sqrt(count_k0 / count_k1)
    k1_dev = translation.shape[0]
    rows = k1_dev // 128
    nboxes = lax.axis_size("box")
    boxes = list_src.shape[0] // nboxes
    me = lax.axis_index("box")
    box_base = me * boxes
    k_base = lax.axis_index("dir") * k1_dev

    pattern = lax.all_gather(radiate(currents, radiation), "dir", axis=0, tiled=True)
    place = lax.all_gather(leaf_place, "dir", axis=0, tiled=True)
    gathered = padded(currents, ((("box", "dir"), 0),), leaf_count)
    local = neighbors - (lax.axis_index(("box", "dir")) - 1) * leaf_count
    near = near_field(gathered, local, block_ids, near_blocks)
    table = jnp.transpose(translation, (2, 1, 0)).reshape(-1, 2, rows, 128)
    part = lax.dynamic_slice_in_dim(interpolation, k_base, k1_dev, 1)
    table_c, table_s, polar_sine = phase_table(k_base, k1_dev, polar)

    named = onehot(list_src.reshape(nboxes, -1), boxes, box_base).max(1)
    slot = onehot(ranks(named).astype(jnp.int32), need) * named[:, :, None]
    slot = jnp.swapaxes(slot, 1, 2).reshape(nboxes * need, boxes)
    mine_src = lax.dynamic_slice_in_dim(list_src, box_base, boxes, 0).reshape(-1)
    mine_off = lax.dynamic_slice_in_dim(list_offset, box_base, boxes, 0).reshape(-1)
    mine_hot = onehot(mine_src, nboxes * boxes)
    wanted = mine_hot.max(0).reshape(nboxes, boxes)
    where = ranks(wanted) + need * jnp.arange(nboxes, dtype=jnp.float32)[:, None]
    mine_index = exact_matmul(mine_hot, where.reshape(-1, 1))[:, 0].astype(jnp.int32)

    parent_hot = onehot(place[:, 0], boxes, box_base)
    position_hot = onehot(place[:, 1], 64)
    cosine = matmul(position_hot, table_c)
    sine = matmul(position_hot, table_s)
    wave_r = matmul(pattern[:, 0], part)
    wave_i = matmul(pattern[:, 1], part)
    shift_r = wave_r * cosine + wave_i * sine
    shift_i = wave_i * cosine - wave_r * sine
    slot_hot = exact_matmul(slot, parent_hot.T)
    send = jnp.stack([matmul(slot_hot, shift_r), matmul(slot_hot, shift_i)], 1)
    send = send.reshape(nboxes, need, 2, rows, 128)
    fields = exchange(send, table, mine_index, mine_off, boxes)
    fields = fields.reshape(boxes, 2, k1_dev)
    field_r = matmul(parent_hot, fields[:, 0])
    field_i = matmul(parent_hot, fields[:, 1])
    weight = polar_sine * scale
    back_r = (field_r * cosine - field_i * sine) * weight
    back_i = (field_r * sine + field_i * cosine) * weight
    far = jnp.stack([matmul(back_r, part.T), matmul(back_i, part.T)], 1)
    far = lax.psum_scatter(far, "dir", scatter_dimension=0, tiled=True)
    return near + receive(far[:, 0], far[:, 1], radiation)


def solution(mesh):
    placed = (
        P(("box", "dir"), None, None),
        P(),
        P(("box", "dir"), None),
        P(("box", "dir"), None),
        P(("box", "dir"), None),
        P(),
        P(),
        P("dir", None, None),
        P(),
        P(),
    )
    return jax.shard_map(
        on_device,
        mesh=mesh,
        in_specs=placed,
        out_specs=P(("box", "dir"), None, None),
        check_vma=False,
    )
```

```python
import functools
import math

import jax
import jax.numpy as jnp
from jax import lax
from jax.experimental import pallas as pl
from jax.experimental.pallas import tpu as pltpu
from jax.sharding import PartitionSpec as P

kappa_leaf = math.pi
need = 8
MESH = pl.DeviceIdType.MESH


def exact_matmul(left, right):
    return jnp.dot(
        left.astype(jnp.bfloat16),
        right.astype(jnp.bfloat16),
        preferred_element_type=jnp.float32,
    )


def onehot(values, count, base=0):
    return ((values - base)[..., None] == jnp.arange(count, dtype=jnp.int32)).astype(jnp.float32)


def axis_factors(start, count, polar, scale):
    order = start + jnp.arange(count, dtype=jnp.int32)
    cycle = order // (2 * polar)
    beside_all = order % (2 * polar)
    theta = math.pi * (cycle.astype(jnp.float32) + 0.5) / polar
    azimuth = math.pi * beside_all.astype(jnp.float32) / polar
    along = jnp.stack(
        [jnp.sin(theta) * jnp.cos(azimuth), jnp.sin(theta) * jnp.sin(azimuth), jnp.cos(theta)]
    )
    near_angle = kappa_leaf * 0.5 * along
    far_angle = kappa_leaf * 1.5 * along
    weight = (jnp.sin(theta) * scale)[None, :]
    return jnp.concatenate(
        [jnp.cos(near_angle), jnp.sin(near_angle), jnp.cos(far_angle), jnp.sin(far_angle)]
        + [weight] * 4
    )


def near_pairs(local, kinds, count, width):
    return jnp.einsum(
        "ljt,ljm->tlm",
        onehot(kinds, count).astype(jnp.bfloat16),
        onehot(local, width).astype(jnp.bfloat16),
        preferred_element_type=jnp.float32,
    ).astype(jnp.bfloat16)


def ranks(present):
    size = present.shape[1]
    order = jnp.arange(size)
    before = (order[:, None] < order[None, :]).astype(jnp.float32)
    return exact_matmul(present, before)


nn = (((1,), (0,)), ((), ()))
nt = (((1,), (1,)), ((), ()))
tn = (((0,), (0,)), ((), ()))


def dot(left, right, dims):
    return lax.dot_general(left, right, dims, preferred_element_type=jnp.float32)


def split(value):
    top = value.astype(jnp.bfloat16)
    return top, (value - top.astype(jnp.float32)).astype(jnp.bfloat16)


def dot3(left, right, dims):
    return dot(left[0], right[0], dims) + (
        dot(left[0], right[1], dims) + dot(left[1], right[0], dims)
    )


def flag(mask):
    return mask.astype(jnp.float32).astype(jnp.bfloat16)


def fmm_kernel(
    peers,
    dirs,
    boxes,
    chunks,
    index_ref,
    off_ref,
    cur_ref,
    place_ref,
    slot_ref,
    axes_ref,
    part_ref,
    table_ref,
    pairs_ref,
    block_ref,
    rad_ref,
    out_ref,
    held_cur,
    part_h,
    part_l,
    cos_tab,
    sin_tab,
    pat_h,
    pat_l,
    cos_ref,
    sin_ref,
    acc_ref,
    near_ref,
    p_ref,
    q_ref,
    far_ref,
    far_in,
    cur_send,
    cur_recv,
    halo_send,
    halo_recv,
    box_send,
    box_recv,
    far_send,
    far_recv,
    *parts,
):
    send = parts[:chunks]
    held = parts[chunks : 2 * chunks]
    swap = parts[2 * chunks : 3 * chunks]
    me = lax.axis_index("box")
    my_dir = lax.axis_index("dir")
    leaves = cur_ref.shape[0] // 2
    width = cur_ref.shape[1]
    k1_dev = part_ref.shape[1]
    size = k1_dev // chunks
    tiles = size // 128
    rows = 2 * tiles
    slots = peers * need
    length = index_ref.shape[0] // boxes
    count = pairs_ref.shape[0]

    held_cur[1 + my_dir, 0:leaves, 0:width] = cur_ref[pl.ds(0, leaves, stride=2), :]
    held_cur[1 + my_dir, 0:leaves, width : 2 * width] = cur_ref[pl.ds(1, leaves, stride=2), :]
    held_cur[1 + my_dir, leaves : leaves + 8, :] = place_ref[...]

    up = jnp.logical_and(my_dir == dirs - 1, me < peers - 1)
    down = jnp.logical_and(my_dir == 0, me > 0)
    barrier = pltpu.get_barrier_semaphore()

    def greet(device):
        pl.semaphore_signal(barrier, inc=1, device_id=device, device_id_type=MESH)

    for step in range(1, peers):
        greet({"box": lax.rem(me + step, peers)})
    for step in range(1, dirs):
        greet({"dir": lax.rem(my_dir + step, dirs)})

    @pl.when(up)
    def _():
        greet((me + 1, 0))

    @pl.when(down)
    def _():
        greet((me - 1, dirs - 1))

    sides = up.astype(jnp.int32) + down.astype(jnp.int32)
    pl.semaphore_wait(barrier, peers + dirs - 2 + sides)

    def remote(source, target, send_sem, recv_sem, device):
        return pltpu.make_async_remote_copy(
            src_ref=source,
            dst_ref=target,
            send_sem=send_sem,
            recv_sem=recv_sem,
            device_id=device,
            device_id_type=MESH,
        )

    cur_copies = []
    for step in range(1, dirs):
        copy = remote(
            held_cur.at[1 + my_dir],
            held_cur.at[1 + my_dir],
            cur_send.at[step],
            cur_recv.at[step],
            {"dir": lax.rem(my_dir + step, dirs)},
        )
        copy.start()
        cur_copies.append(copy)

    def halo_up():
        return remote(
            held_cur.at[1 + my_dir], held_cur.at[0], halo_send.at[0], halo_recv.at[0], (me + 1, 0)
        )

    def halo_down():
        return remote(
            held_cur.at[1 + my_dir],
            held_cur.at[dirs + 1],
            halo_send.at[1],
            halo_recv.at[1],
            (me - 1, dirs - 1),
        )

    @pl.when(up)
    def _():
        halo_up().start()

    @pl.when(down)
    def _():
        halo_down().start()

    top, low = split(part_ref[...])
    part_h[...] = top
    part_l[...] = low

    def table_chunk(chunk):
        cols = pl.ds(chunk * size, size)
        position = lax.broadcasted_iota(jnp.int32, (64, size), 0)

        def factor(which, axis):
            inner = jnp.logical_or(which == 1, which == 2)
            cosine = jnp.where(inner, axes_ref[axis : axis + 1, cols], axes_ref[6 + axis : 7 + axis, cols])
            sine = jnp.where(inner, axes_ref[3 + axis : 4 + axis, cols], axes_ref[9 + axis : 10 + axis, cols])
            return cosine, jnp.where(which < 2, -sine, sine)

        x_c, x_s = factor(position % 4, 0)
        y_c, y_s = factor(position // 4 % 4, 1)
        z_c, z_s = factor(position // 16, 2)
        xy_c = x_c * y_c - x_s * y_s
        xy_s = x_c * y_s + x_s * y_c
        cos_h, cos_l = split(xy_c * z_c - xy_s * z_s)
        sin_h, sin_l = split(xy_c * z_s + xy_s * z_c)
        cos_tab[0:64, cols] = cos_h
        cos_tab[64:128, cols] = cos_l
        sin_tab[0:64, cols] = sin_h
        sin_tab[64:128, cols] = sin_l

    for chunk in range(chunks):
        table_chunk(chunk)

    rad_r = split(rad_ref[0])
    rad_i = split(rad_ref[1])
    for copy in cur_copies:
        copy.wait()

    def patterns(d, carry):
        cur_r = split(held_cur[1 + d, 0:leaves, 0:width])
        cur_i = split(held_cur[1 + d, 0:leaves, width : 2 * width])
        real = dot3(cur_r, rad_r, nn) - dot3(cur_i, rad_i, nn)
        imag = dot3(cur_r, rad_i, nn) + dot3(cur_i, rad_r, nn)
        top, low = split(real)
        pat_h[d, 0:leaves] = top
        pat_l[d, 0:leaves] = low
        top, low = split(imag)
        pat_h[d, leaves : 2 * leaves] = top
        pat_l[d, leaves : 2 * leaves] = low
        return carry

    lax.fori_loop(0, dirs, patterns, 0)

    def block(owner):
        return pl.ds(pl.multiple_of(owner * (need * rows), need * rows), need * rows)

    box_copies = []
    for chunk in range(chunks):
        cols = pl.ds(chunk * size, size)
        acc_ref[...] = jnp.zeros_like(acc_ref)

        def outgoing(d, carry):
            wave = dot3((pat_h[d], pat_l[d]), (part_h[:, cols], part_l[:, cols]), nn)
            wave_r = wave[0:leaves]
            wave_i = wave[leaves : 2 * leaves]
            parent = held_cur[1 + d, leaves : leaves + 1, 0:width]
            place = held_cur[1 + d, leaves : leaves + 1, width : 2 * width]
            order = lax.broadcasted_iota(jnp.int32, (128, leaves), 0) % 64
            hot = flag(order.astype(jnp.float32) == place)
            cosine = dot(hot, cos_tab[:, cols], tn)
            sine = dot(hot, sin_tab[:, cols], tn)
            cos_ref[d, :, cols] = cosine
            sin_ref[d, :, cols] = sine
            slot_hot = flag(slot_ref[...] == parent)
            for part, value in enumerate(
                (wave_r * cosine + wave_i * sine, wave_i * cosine - wave_r * sine)
            ):
                top, low = split(value)
                acc_ref[part] += dot(slot_hot, top, nn) + dot(slot_hot, low, nn)
            return carry

        lax.fori_loop(0, dirs, outgoing, 0)
        for tile in range(tiles):
            for part in range(2):
                send[chunk][pl.ds(2 * tile + part, slots, stride=rows), :] = acc_ref[
                    part, :, tile * 128 : (tile + 1) * 128
                ]
        copies = []
        for step in range(1, peers):
            other = lax.rem(me + step, peers)
            copy = remote(
                send[chunk].at[block(other)],
                held[chunk].at[block(me)],
                box_send.at[chunk, step],
                box_recv.at[chunk, step],
                {"box": other},
            )
            copy.start()
            copies.append(copy)
        box_copies.append(copies)
        held[chunk][block(me), :] = send[chunk][block(me), :]

    @pl.when(up)
    def _():
        halo_up().wait_send()

    @pl.when(down)
    def _():
        halo_down().wait_send()

    @pl.when(down)
    def _():
        halo_up().wait_recv()

    @pl.when(up)
    def _():
        halo_down().wait_recv()

    @pl.when(me == 0)
    def _():
        held_cur[0] = jnp.zeros(held_cur.shape[1:], jnp.float32)

    @pl.when(me == peers - 1)
    def _():
        held_cur[dirs + 1] = jnp.zeros(held_cur.shape[1:], jnp.float32)

    around = jnp.concatenate([held_cur[my_dir + side, 0:leaves, :] for side in range(3)], axis=0)
    around_h, around_l = split(around)
    near_ref[...] = jnp.zeros_like(near_ref)

    def near(t, carry):
        summed = dot(pairs_ref[t], around_h, nn) + dot(pairs_ref[t], around_l, nn)
        stacked = split(jnp.concatenate([summed[:, 0:width], summed[:, width : 2 * width]], axis=0))
        by_r = dot3(stacked, split(block_ref[t, 0]), nt)
        by_i = dot3(stacked, split(block_ref[t, 1]), nt)
        near_ref[0] += by_r[0:leaves] - by_i[leaves : 2 * leaves]
        near_ref[1] += by_r[leaves : 2 * leaves] + by_i[0:leaves]
        return carry

    lax.fori_loop(0, count, near, 0)
    far_ref[...] = jnp.zeros_like(far_ref)

    for chunk in range(chunks):
        cols = pl.ds(chunk * size, size)
        for copy in box_copies[chunk]:
            copy.wait()
        got = held[chunk]
        other = swap[chunk]

        def turn(slot, carry):
            where = pl.ds(pl.multiple_of(slot * rows, rows), rows)
            value = got[where, :]
            odd = lax.broadcasted_iota(jnp.int32, value.shape, 0) % 2
            other[slot, 0] = value
            other[slot, 1] = jnp.where(
                odd == 0, pltpu.roll(value, rows - 1, 0), pltpu.roll(value, 1, 0)
            )
            return carry

        lax.fori_loop(0, slots, turn, 0, unroll=4)

        def translate(box, carry):
            def entry(item, total):
                along, across = total
                source = index_ref[box * length + item]
                table = table_ref[off_ref[box * length + item], chunk]
                return along + table * other[source, 0], across + table * other[source, 1]

            zero = jnp.zeros((rows, 128), jnp.float32)
            along, across = lax.fori_loop(0, length, entry, (zero, zero), unroll=8)
            where = pl.ds(pl.multiple_of(box * rows, rows), rows)
            p_ref[where, :] = along
            q_ref[where, :] = across
            return carry

        lax.fori_loop(0, boxes, translate, 0)

        def pick(ref, row):
            return ref[pl.ds(row, boxes, stride=rows), :]

        field_r = jnp.concatenate(
            [pick(p_ref, 2 * tile) - pick(p_ref, 2 * tile + 1) for tile in range(tiles)], axis=1
        )
        field_i = jnp.concatenate(
            [pick(q_ref, 2 * tile) + pick(q_ref, 2 * tile + 1) for tile in range(tiles)], axis=1
        )
        field_r = jnp.concatenate(split(field_r), axis=0)
        field_i = jnp.concatenate(split(field_i), axis=0)

        def incoming(d, carry):
            parent = held_cur[1 + d, leaves : leaves + 1, 0:width]
            order = lax.broadcasted_iota(jnp.int32, (2 * boxes, leaves), 0) % boxes + me * boxes
            hot = flag(order.astype(jnp.float32) == parent)
            real = dot(hot, field_r, tn)
            imag = dot(hot, field_i, tn)
            cosine = cos_ref[d, :, cols]
            sine = sin_ref[d, :, cols]
            weight = axes_ref[12:13, cols]
            back = (part_h[:, cols], part_l[:, cols])
            far_ref[d, 0:leaves] += dot3(split((real * cosine - imag * sine) * weight), back, nt)
            far_ref[d, leaves : 2 * leaves] += dot3(
                split((real * sine + imag * cosine) * weight), back, nt
            )
            return carry

        lax.fori_loop(0, dirs, incoming, 0)

    copies = []
    for step in range(1, dirs):
        other_dir = lax.rem(my_dir + step, dirs)
        copy = remote(
            far_ref.at[other_dir],
            far_in.at[step],
            far_send.at[step],
            far_recv.at[step],
            {"dir": other_dir},
        )
        copy.start()
        copies.append(copy)
    far = far_ref[my_dir]
    for step, copy in enumerate(copies):
        copy.wait()
        far = far + far_in[step + 1]
    far = split(far)
    by_r = dot3(far, rad_r, nt)
    by_i = dot3(far, rad_i, nt)
    out_ref[pl.ds(0, leaves, stride=2), :] = near_ref[0] + by_r[0:leaves] + by_i[leaves : 2 * leaves]
    out_ref[pl.ds(1, leaves, stride=2), :] = near_ref[1] + by_r[leaves : 2 * leaves] - by_i[0:leaves]


def fmm(peers, dirs, boxes, index, offsets, *arrays):
    cur, place, slots, axes, part, table, pairs, blocks, radiation = arrays
    k0, k1_dev = part.shape
    chunks = max(1, k1_dev // 1024)
    size = k1_dev // chunks
    rows = 2 * size // 128
    leaves = cur.shape[0] // 2
    exchanged = pltpu.VMEM((peers * need * rows, 128), jnp.float32)
    dma = pltpu.SemaphoreType.DMA
    vmem = pl.BlockSpec(memory_space=pltpu.VMEM)
    smem = pl.BlockSpec(memory_space=pltpu.SMEM)
    f32 = jnp.float32
    bf16 = jnp.bfloat16
    return pl.pallas_call(
        functools.partial(fmm_kernel, peers, dirs, boxes, chunks),
        out_shape=jax.ShapeDtypeStruct(cur.shape, f32),
        in_specs=[smem, smem] + [vmem] * len(arrays),
        out_specs=vmem,
        scratch_shapes=[
            pltpu.VMEM((dirs + 2, leaves + 8, 2 * cur.shape[1]), f32),
            pltpu.VMEM((k0, k1_dev), bf16),
            pltpu.VMEM((k0, k1_dev), bf16),
            pltpu.VMEM((128, k1_dev), bf16),
            pltpu.VMEM((128, k1_dev), bf16),
            pltpu.VMEM((dirs, 2 * leaves, k0), bf16),
            pltpu.VMEM((dirs, 2 * leaves, k0), bf16),
            pltpu.VMEM((dirs, leaves, k1_dev), f32),
            pltpu.VMEM((dirs, leaves, k1_dev), f32),
            pltpu.VMEM((2, peers * need, size), f32),
            pltpu.VMEM((2, leaves, cur.shape[1]), f32),
            pltpu.VMEM((boxes * rows, 128), f32),
            pltpu.VMEM((boxes * rows, 128), f32),
            pltpu.VMEM((dirs, 2 * leaves, k0), f32),
            pltpu.VMEM((dirs, 2 * leaves, k0), f32),
            dma((dirs,)),
            dma((dirs,)),
            dma((2,)),
            dma((2,)),
            dma((chunks, peers)),
            dma((chunks, peers)),
            dma((dirs,)),
            dma((dirs,)),
        ]
        + [exchanged] * (2 * chunks)
        + [pltpu.VMEM((peers * need, 2, rows, 128), f32)] * chunks,
        compiler_params=pltpu.CompilerParams(
            collective_id=0, has_side_effects=True, vmem_limit_bytes=50 * 2**20
        ),
    )(index, offsets, *arrays)


def on_device(
    currents,
    near_blocks,
    block_ids,
    neighbors,
    leaf_place,
    radiation,
    interpolation,
    translation,
    list_src,
    list_offset,
):
    leaf_count = currents.shape[0]
    count_k0 = interpolation.shape[0]
    count_k1 = interpolation.shape[1]
    polar = math.isqrt(count_k1 // 2)
    scale = math.sqrt(count_k0 / count_k1)
    k1_dev = translation.shape[0]
    rows = k1_dev // 128
    nboxes = lax.axis_size("box")
    boxes = list_src.shape[0] // nboxes
    me = lax.axis_index("box")
    box_base = me * boxes
    k_base = lax.axis_index("dir") * k1_dev

    local = neighbors - (lax.axis_index(("box", "dir")) - 1) * leaf_count
    pairs = near_pairs(local, block_ids, near_blocks.shape[0], 3 * leaf_count)
    table = jnp.transpose(translation, (2, 1, 0)).reshape(-1, 2, rows, 128)
    chunks = max(1, k1_dev // 1024)
    table = jnp.swapaxes(table, 1, 2).reshape(-1, chunks, 2 * rows // chunks, 128)
    part = lax.dynamic_slice_in_dim(interpolation, k_base, k1_dev, 1)
    axes = axis_factors(k_base, k1_dev, polar, scale)
    place = jnp.broadcast_to(leaf_place.T.astype(jnp.float32).reshape(1, -1), (8, 2 * leaf_count))

    named = onehot(list_src.reshape(nboxes, -1), boxes, box_base).max(1)
    slot = onehot(ranks(named).astype(jnp.int32), need) * named[:, :, None]
    slot = jnp.swapaxes(slot, 1, 2).reshape(nboxes * need, boxes)
    mine_src = lax.dynamic_slice_in_dim(list_src, box_base, boxes, 0).reshape(-1)
    mine_off = lax.dynamic_slice_in_dim(list_offset, box_base, boxes, 0).reshape(-1)
    mine_hot = onehot(mine_src, nboxes * boxes)
    wanted = mine_hot.max(0).reshape(nboxes, boxes)
    where = ranks(wanted) + need * jnp.arange(nboxes, dtype=jnp.float32)[:, None]
    mine_index = exact_matmul(mine_hot, where.reshape(-1, 1))[:, 0].astype(jnp.int32)

    named_box = exact_matmul(slot, jnp.arange(boxes, dtype=jnp.float32)[:, None]) + (
        box_base.astype(jnp.float32)
    )
    slots = jnp.broadcast_to(named_box, (nboxes * need, leaf_count))
    out = fmm(
        nboxes,
        lax.axis_size("dir"),
        boxes,
        mine_index,
        mine_off,
        currents.reshape(2 * leaf_count, -1),
        place,
        slots,
        axes,
        part,
        table,
        pairs,
        near_blocks,
        radiation,
    )
    return out.reshape(currents.shape)


def solution(mesh):
    placed = (
        P(("box", "dir"), None, None),
        P(),
        P(("box", "dir"), None),
        P(("box", "dir"), None),
        P(("box", "dir"), None),
        P(),
        P(),
        P("dir", None, None),
        P(),
        P(),
    )
    return jax.shard_map(
        on_device,
        mesh=mesh,
        in_specs=placed,
        out_specs=P(("box", "dir"), None, None),
        check_vma=False,
    )
```

```python
import functools
import math

import jax
import jax.numpy as jnp
from jax import lax
from jax.experimental import pallas as pl
from jax.experimental.pallas import tpu as pltpu
from jax.sharding import PartitionSpec as P

kappa_leaf = math.pi
need = 8
MESH = pl.DeviceIdType.MESH


def exact_matmul(left, right):
    return jnp.dot(
        left.astype(jnp.bfloat16),
        right.astype(jnp.bfloat16),
        preferred_element_type=jnp.float32,
    )


def onehot(values, count, base=0):
    return ((values - base)[..., None] == jnp.arange(count, dtype=jnp.int32)).astype(jnp.float32)


def axis_factors(start, count, polar, scale):
    order = start + jnp.arange(count, dtype=jnp.int32)
    cycle = order // (2 * polar)
    beside_all = order % (2 * polar)
    theta = math.pi * (cycle.astype(jnp.float32) + 0.5) / polar
    azimuth = math.pi * beside_all.astype(jnp.float32) / polar
    along = jnp.stack(
        [jnp.sin(theta) * jnp.cos(azimuth), jnp.sin(theta) * jnp.sin(azimuth), jnp.cos(theta)]
    )
    near_angle = kappa_leaf * 0.5 * along
    far_angle = kappa_leaf * 1.5 * along
    weight = (jnp.sin(theta) * scale)[None, :]
    return jnp.concatenate(
        [jnp.cos(near_angle), jnp.sin(near_angle), jnp.cos(far_angle), jnp.sin(far_angle)]
        + [weight] * 4
    )


def near_pairs(local, kinds, count, width):
    return jnp.einsum(
        "ljt,ljm->tlm",
        onehot(kinds, count).astype(jnp.bfloat16),
        onehot(local, width).astype(jnp.bfloat16),
        preferred_element_type=jnp.float32,
    ).astype(jnp.bfloat16)


def ranks(present):
    size = present.shape[1]
    order = jnp.arange(size)
    before = (order[:, None] < order[None, :]).astype(jnp.float32)
    return exact_matmul(present, before)


nn = (((1,), (0,)), ((), ()))
nt = (((1,), (1,)), ((), ()))
tn = (((0,), (0,)), ((), ()))


def dot(left, right, dims):
    return lax.dot_general(left, right, dims, preferred_element_type=jnp.float32)


def split(value):
    top = value.astype(jnp.bfloat16)
    return top, (value - top.astype(jnp.float32)).astype(jnp.bfloat16)


def dot3(left, right, dims):
    return dot(left[0], right[0], dims) + (
        dot(left[0], right[1], dims) + dot(left[1], right[0], dims)
    )


def flag(mask):
    return mask.astype(jnp.float32).astype(jnp.bfloat16)


def fmm_kernel(
    peers,
    dirs,
    boxes,
    chunks,
    index_ref,
    off_ref,
    cur_ref,
    place_ref,
    slot_ref,
    axes_ref,
    part_hbm,
    table_hbm,
    pairs_ref,
    block_hbm,
    rad_ref,
    out_ref,
    part_ref,
    table_ref,
    block_ref,
    load_sem,
    held_cur,
    part_h,
    part_l,
    cos_tab,
    sin_tab,
    pat_h,
    pat_l,
    cos_ref,
    sin_ref,
    acc_ref,
    near_ref,
    p_ref,
    q_ref,
    far_ref,
    far_in,
    cur_send,
    cur_recv,
    halo_send,
    halo_recv,
    box_send,
    box_recv,
    far_send,
    far_recv,
    *parts,
):
    send = parts[:chunks]
    held = parts[chunks : 2 * chunks]
    swap = parts[2 * chunks : 3 * chunks]
    me = lax.axis_index("box")
    my_dir = lax.axis_index("dir")
    leaves = cur_ref.shape[0] // 2
    width = cur_ref.shape[1]
    k1_dev = part_ref.shape[1]
    size = k1_dev // chunks
    tiles = size // 128
    rows = 2 * tiles
    slots = peers * need
    length = index_ref.shape[0] // boxes
    count = pairs_ref.shape[0]

    part_cols = pl.ds(pl.multiple_of(my_dir * k1_dev, k1_dev), k1_dev)
    load_part = pltpu.make_async_copy(part_hbm.at[:, part_cols], part_ref, load_sem.at[0])
    load_block = pltpu.make_async_copy(block_hbm, block_ref, load_sem.at[1])
    load_table = pltpu.make_async_copy(table_hbm, table_ref, load_sem.at[2])
    load_part.start()
    load_block.start()
    load_table.start()
    held_cur[1 + my_dir, 0:leaves, 0:width] = cur_ref[pl.ds(0, leaves, stride=2), :]
    held_cur[1 + my_dir, 0:leaves, width : 2 * width] = cur_ref[pl.ds(1, leaves, stride=2), :]
    held_cur[1 + my_dir, leaves : leaves + 8, :] = place_ref[...]

    up = jnp.logical_and(my_dir == dirs - 1, me < peers - 1)
    down = jnp.logical_and(my_dir == 0, me > 0)
    barrier = pltpu.get_barrier_semaphore()

    def greet(device):
        pl.semaphore_signal(barrier, inc=1, device_id=device, device_id_type=MESH)

    for step in range(1, peers):
        greet({"box": lax.rem(me + step, peers)})
    for step in range(1, dirs):
        greet({"dir": lax.rem(my_dir + step, dirs)})

    @pl.when(up)
    def _():
        greet((me + 1, 0))

    @pl.when(down)
    def _():
        greet((me - 1, dirs - 1))

    sides = up.astype(jnp.int32) + down.astype(jnp.int32)
    pl.semaphore_wait(barrier, peers + dirs - 2 + sides)

    def remote(source, target, send_sem, recv_sem, device):
        return pltpu.make_async_remote_copy(
            src_ref=source,
            dst_ref=target,
            send_sem=send_sem,
            recv_sem=recv_sem,
            device_id=device,
            device_id_type=MESH,
        )

    cur_copies = []
    for step in range(1, dirs):
        copy = remote(
            held_cur.at[1 + my_dir],
            held_cur.at[1 + my_dir],
            cur_send.at[step],
            cur_recv.at[step],
            {"dir": lax.rem(my_dir + step, dirs)},
        )
        copy.start()
        cur_copies.append(copy)

    def halo_up():
        return remote(
            held_cur.at[1 + my_dir], held_cur.at[0], halo_send.at[0], halo_recv.at[0], (me + 1, 0)
        )

    def halo_down():
        return remote(
            held_cur.at[1 + my_dir],
            held_cur.at[dirs + 1],
            halo_send.at[1],
            halo_recv.at[1],
            (me - 1, dirs - 1),
        )

    @pl.when(up)
    def _():
        halo_up().start()

    @pl.when(down)
    def _():
        halo_down().start()

    load_part.wait()
    top, low = split(part_ref[...])
    part_h[...] = top
    part_l[...] = low

    def table_chunk(chunk):
        cols = pl.ds(chunk * size, size)
        position = lax.broadcasted_iota(jnp.int32, (64, size), 0)

        def factor(which, axis):
            inner = jnp.logical_or(which == 1, which == 2)
            cosine = jnp.where(inner, axes_ref[axis : axis + 1, cols], axes_ref[6 + axis : 7 + axis, cols])
            sine = jnp.where(inner, axes_ref[3 + axis : 4 + axis, cols], axes_ref[9 + axis : 10 + axis, cols])
            return cosine, jnp.where(which < 2, -sine, sine)

        x_c, x_s = factor(position % 4, 0)
        y_c, y_s = factor(position // 4 % 4, 1)
        z_c, z_s = factor(position // 16, 2)
        xy_c = x_c * y_c - x_s * y_s
        xy_s = x_c * y_s + x_s * y_c
        cos_h, cos_l = split(xy_c * z_c - xy_s * z_s)
        sin_h, sin_l = split(xy_c * z_s + xy_s * z_c)
        cos_tab[0:64, cols] = cos_h
        cos_tab[64:128, cols] = cos_l
        sin_tab[0:64, cols] = sin_h
        sin_tab[64:128, cols] = sin_l

    for chunk in range(chunks):
        table_chunk(chunk)

    rad_r = split(rad_ref[0])
    rad_i = split(rad_ref[1])
    acc_ref[...] = jnp.zeros_like(acc_ref)

    def patterns(d):
        cur_r = split(held_cur[1 + d, 0:leaves, 0:width])
        cur_i = split(held_cur[1 + d, 0:leaves, width : 2 * width])
        real = dot3(cur_r, rad_r, nn) - dot3(cur_i, rad_i, nn)
        imag = dot3(cur_r, rad_i, nn) + dot3(cur_i, rad_r, nn)
        top, low = split(real)
        pat_h[d, 0:leaves] = top
        pat_l[d, 0:leaves] = low
        top, low = split(imag)
        pat_h[d, leaves : 2 * leaves] = top
        pat_l[d, leaves : 2 * leaves] = low

    def block(owner):
        return pl.ds(pl.multiple_of(owner * (need * rows), need * rows), need * rows)

    def outgoing(d, chunk):
        cols = pl.ds(chunk * size, size)
        wave = dot3((pat_h[d], pat_l[d]), (part_h[:, cols], part_l[:, cols]), nn)
        wave_r = wave[0:leaves]
        wave_i = wave[leaves : 2 * leaves]
        parent = held_cur[1 + d, leaves : leaves + 1, 0:width]
        place = held_cur[1 + d, leaves : leaves + 1, width : 2 * width]
        order = lax.broadcasted_iota(jnp.int32, (128, leaves), 0) % 64
        hot = flag(order.astype(jnp.float32) == place)
        cosine = dot(hot, cos_tab[:, cols], tn)
        sine = dot(hot, sin_tab[:, cols], tn)
        cos_ref[d, :, cols] = cosine
        sin_ref[d, :, cols] = sine
        slot_hot = flag(slot_ref[...] == parent)
        for part, value in enumerate(
            (wave_r * cosine + wave_i * sine, wave_i * cosine - wave_r * sine)
        ):
            top, low = split(value)
            acc_ref[chunk, part] += dot(slot_hot, top, nn) + dot(slot_hot, low, nn)

    patterns(my_dir)
    for chunk in range(chunks):
        outgoing(my_dir, chunk)
    for copy in cur_copies:
        copy.wait()

    box_copies = []
    for chunk in range(chunks):

        def others(step, carry):
            d = lax.rem(my_dir + step, dirs)
            if chunk == 0:
                patterns(d)
            outgoing(d, chunk)
            return carry

        lax.fori_loop(1, dirs, others, 0)
        for tile in range(tiles):
            for part in range(2):
                send[chunk][pl.ds(2 * tile + part, slots, stride=rows), :] = acc_ref[
                    chunk, part, :, tile * 128 : (tile + 1) * 128
                ]
        copies = []
        for step in range(1, peers):
            other = lax.rem(me + step, peers)
            copy = remote(
                send[chunk].at[block(other)],
                held[chunk].at[block(me)],
                box_send.at[chunk, step],
                box_recv.at[chunk, step],
                {"box": other},
            )
            copy.start()
            copies.append(copy)
        box_copies.append(copies)
        held[chunk][block(me), :] = send[chunk][block(me), :]

    @pl.when(up)
    def _():
        halo_up().wait_send()

    @pl.when(down)
    def _():
        halo_down().wait_send()

    @pl.when(down)
    def _():
        halo_up().wait_recv()

    @pl.when(up)
    def _():
        halo_down().wait_recv()

    @pl.when(me == 0)
    def _():
        held_cur[0] = jnp.zeros(held_cur.shape[1:], jnp.float32)

    @pl.when(me == peers - 1)
    def _():
        held_cur[dirs + 1] = jnp.zeros(held_cur.shape[1:], jnp.float32)

    around = jnp.concatenate([held_cur[my_dir + side, 0:leaves, :] for side in range(3)], axis=0)
    around_h, around_l = split(around)
    near_ref[...] = jnp.zeros_like(near_ref)

    def near(t, carry):
        summed = dot(pairs_ref[t], around_h, nn) + dot(pairs_ref[t], around_l, nn)
        stacked = split(jnp.concatenate([summed[:, 0:width], summed[:, width : 2 * width]], axis=0))
        by_r = dot3(stacked, split(block_ref[t, 0]), nt)
        by_i = dot3(stacked, split(block_ref[t, 1]), nt)
        near_ref[0] += by_r[0:leaves] - by_i[leaves : 2 * leaves]
        near_ref[1] += by_r[leaves : 2 * leaves] + by_i[0:leaves]
        return carry

    load_block.wait()
    lax.fori_loop(0, count // 2, near, 0)
    load_table.wait()
    far_ref[...] = jnp.zeros_like(far_ref)

    for chunk in range(chunks):
        cols = pl.ds(chunk * size, size)
        for copy in box_copies[chunk]:
            copy.wait()
        got = held[chunk]
        other = swap[chunk]

        def turn(slot, carry):
            where = pl.ds(pl.multiple_of(slot * rows, rows), rows)
            value = got[where, :]
            odd = lax.broadcasted_iota(jnp.int32, value.shape, 0) % 2
            other[slot, 0] = value
            other[slot, 1] = jnp.where(
                odd == 0, pltpu.roll(value, rows - 1, 0), pltpu.roll(value, 1, 0)
            )
            return carry

        lax.fori_loop(0, slots, turn, 0, unroll=4)

        def translate(box, carry):
            def entry(item, total):
                along, across = total
                source = index_ref[box * length + item]
                table = table_ref[off_ref[box * length + item], chunk]
                return along + table * other[source, 0], across + table * other[source, 1]

            zero = jnp.zeros((rows, 128), jnp.float32)
            along, across = lax.fori_loop(0, length, entry, (zero, zero), unroll=8)
            where = pl.ds(pl.multiple_of(box * rows, rows), rows)
            p_ref[where, :] = along
            q_ref[where, :] = across
            return carry

        lax.fori_loop(0, boxes, translate, 0)

        def pick(ref, row):
            return ref[pl.ds(row, boxes, stride=rows), :]

        field_r = jnp.concatenate(
            [pick(p_ref, 2 * tile) - pick(p_ref, 2 * tile + 1) for tile in range(tiles)], axis=1
        )
        field_i = jnp.concatenate(
            [pick(q_ref, 2 * tile) + pick(q_ref, 2 * tile + 1) for tile in range(tiles)], axis=1
        )
        field_r = jnp.concatenate(split(field_r), axis=0)
        field_i = jnp.concatenate(split(field_i), axis=0)

        def incoming(d):
            parent = held_cur[1 + d, leaves : leaves + 1, 0:width]
            order = lax.broadcasted_iota(jnp.int32, (2 * boxes, leaves), 0) % boxes + me * boxes
            hot = flag(order.astype(jnp.float32) == parent)
            real = dot(hot, field_r, tn)
            imag = dot(hot, field_i, tn)
            cosine = cos_ref[d, :, cols]
            sine = sin_ref[d, :, cols]
            weight = axes_ref[12:13, cols]
            back = (part_h[:, cols], part_l[:, cols])
            far_ref[d, 0:leaves] += dot3(split((real * cosine - imag * sine) * weight), back, nt)
            far_ref[d, leaves : 2 * leaves] += dot3(
                split((real * sine + imag * cosine) * weight), back, nt
            )

        def all_incoming(d, carry):
            incoming(d)
            return carry

        if chunk < chunks - 1:
            lax.fori_loop(0, dirs, all_incoming, 0)

    copies = []
    for step in range(1, dirs):
        other_dir = lax.rem(my_dir + step, dirs)
        incoming(other_dir)
        copy = remote(
            far_ref.at[other_dir],
            far_in.at[step],
            far_send.at[step],
            far_recv.at[step],
            {"dir": other_dir},
        )
        copy.start()
        copies.append(copy)
    incoming(my_dir)
    lax.fori_loop(count // 2, count, near, 0)
    far = far_ref[my_dir]
    for step, copy in enumerate(copies):
        copy.wait()
        far = far + far_in[step + 1]
    far = split(far)
    by_r = dot3(far, rad_r, nt)
    by_i = dot3(far, rad_i, nt)
    out_ref[pl.ds(0, leaves, stride=2), :] = near_ref[0] + by_r[0:leaves] + by_i[leaves : 2 * leaves]
    out_ref[pl.ds(1, leaves, stride=2), :] = near_ref[1] + by_r[leaves : 2 * leaves] - by_i[0:leaves]


def fmm(peers, dirs, boxes, index, offsets, *arrays):
    cur, place, slots, axes, part, table, pairs, blocks, radiation = arrays
    k0 = part.shape[0]
    k1_dev = part.shape[1] // dirs
    chunks = max(1, k1_dev // 1024)
    size = k1_dev // chunks
    rows = 2 * size // 128
    leaves = cur.shape[0] // 2
    exchanged = pltpu.VMEM((peers * need * rows, 128), jnp.float32)
    dma = pltpu.SemaphoreType.DMA
    vmem = pl.BlockSpec(memory_space=pltpu.VMEM)
    smem = pl.BlockSpec(memory_space=pltpu.SMEM)
    hbm = pl.BlockSpec(memory_space=pl.ANY)
    f32 = jnp.float32
    bf16 = jnp.bfloat16
    return pl.pallas_call(
        functools.partial(fmm_kernel, peers, dirs, boxes, chunks),
        out_shape=jax.ShapeDtypeStruct(cur.shape, f32),
        in_specs=[smem, smem] + [vmem] * 4 + [hbm, hbm, vmem, hbm, vmem],
        out_specs=vmem,
        scratch_shapes=[
            pltpu.VMEM((k0, k1_dev), f32),
            pltpu.VMEM(table.shape, f32),
            pltpu.VMEM(blocks.shape, f32),
            dma((3,)),
            pltpu.VMEM((dirs + 2, leaves + 8, 2 * cur.shape[1]), f32),
            pltpu.VMEM((k0, k1_dev), bf16),
            pltpu.VMEM((k0, k1_dev), bf16),
            pltpu.VMEM((128, k1_dev), bf16),
            pltpu.VMEM((128, k1_dev), bf16),
            pltpu.VMEM((dirs, 2 * leaves, k0), bf16),
            pltpu.VMEM((dirs, 2 * leaves, k0), bf16),
            pltpu.VMEM((dirs, leaves, k1_dev), f32),
            pltpu.VMEM((dirs, leaves, k1_dev), f32),
            pltpu.VMEM((chunks, 2, peers * need, size), f32),
            pltpu.VMEM((2, leaves, cur.shape[1]), f32),
            pltpu.VMEM((boxes * rows, 128), f32),
            pltpu.VMEM((boxes * rows, 128), f32),
            pltpu.VMEM((dirs, 2 * leaves, k0), f32),
            pltpu.VMEM((dirs, 2 * leaves, k0), f32),
            dma((dirs,)),
            dma((dirs,)),
            dma((2,)),
            dma((2,)),
            dma((chunks, peers)),
            dma((chunks, peers)),
            dma((dirs,)),
            dma((dirs,)),
        ]
        + [exchanged] * (2 * chunks)
        + [pltpu.VMEM((peers * need, 2, rows, 128), f32)] * chunks,
        compiler_params=pltpu.CompilerParams(
            collective_id=0, has_side_effects=True, vmem_limit_bytes=50 * 2**20
        ),
    )(index, offsets, *arrays)


def on_device(
    currents,
    near_blocks,
    block_ids,
    neighbors,
    leaf_place,
    radiation,
    interpolation,
    translation,
    list_src,
    list_offset,
):
    leaf_count = currents.shape[0]
    count_k0 = interpolation.shape[0]
    count_k1 = interpolation.shape[1]
    polar = math.isqrt(count_k1 // 2)
    scale = math.sqrt(count_k0 / count_k1)
    k1_dev = translation.shape[0]
    rows = k1_dev // 128
    nboxes = lax.axis_size("box")
    boxes = list_src.shape[0] // nboxes
    me = lax.axis_index("box")
    box_base = me * boxes
    k_base = lax.axis_index("dir") * k1_dev

    local = neighbors - (lax.axis_index(("box", "dir")) - 1) * leaf_count
    pairs = near_pairs(local, block_ids, near_blocks.shape[0], 3 * leaf_count)
    table = jnp.transpose(translation, (2, 1, 0)).reshape(-1, 2, rows, 128)
    chunks = max(1, k1_dev // 1024)
    table = jnp.swapaxes(table, 1, 2).reshape(-1, chunks, 2 * rows // chunks, 128)
    axes = axis_factors(k_base, k1_dev, polar, scale)
    place = jnp.broadcast_to(leaf_place.T.astype(jnp.float32).reshape(1, -1), (8, 2 * leaf_count))

    named = onehot(list_src.reshape(nboxes, -1), boxes, box_base).max(1)
    slot = onehot(ranks(named).astype(jnp.int32), need) * named[:, :, None]
    slot = jnp.swapaxes(slot, 1, 2).reshape(nboxes * need, boxes)
    mine_src = lax.dynamic_slice_in_dim(list_src, box_base, boxes, 0).reshape(-1)
    mine_off = lax.dynamic_slice_in_dim(list_offset, box_base, boxes, 0).reshape(-1)
    mine_hot = onehot(mine_src, nboxes * boxes)
    wanted = mine_hot.max(0).reshape(nboxes, boxes)
    where = ranks(wanted) + need * jnp.arange(nboxes, dtype=jnp.float32)[:, None]
    mine_index = exact_matmul(mine_hot, where.reshape(-1, 1))[:, 0].astype(jnp.int32)

    named_box = exact_matmul(slot, jnp.arange(boxes, dtype=jnp.float32)[:, None]) + (
        box_base.astype(jnp.float32)
    )
    slots = jnp.broadcast_to(named_box, (nboxes * need, leaf_count))
    out = fmm(
        nboxes,
        lax.axis_size("dir"),
        boxes,
        mine_index,
        mine_off,
        currents.reshape(2 * leaf_count, -1),
        place,
        slots,
        axes,
        interpolation,
        table,
        pairs,
        near_blocks,
        radiation,
    )
    return out.reshape(currents.shape)


def solution(mesh):
    placed = (
        P(("box", "dir"), None, None),
        P(),
        P(("box", "dir"), None),
        P(("box", "dir"), None),
        P(("box", "dir"), None),
        P(),
        P(),
        P("dir", None, None),
        P(),
        P(),
    )
    return jax.shard_map(
        on_device,
        mesh=mesh,
        in_specs=placed,
        out_specs=P(("box", "dir"), None, None),
        check_vma=False,
    )
```
